32 devices in a mesh: req: 16 (over z, x, core), tp: 2 (over y).
Axes of the slice: x: 2, y: 2, z: 4, core: 2. Of those that a mesh axis runs over, the one named last changes fastest.
Arguments:
- queries: bfloat16 [2048, 8192], P('req', 'tp'), may hold values from -16 to 16
- span_rotated_keys: bfloat16 [2048, 1024], P('req', 'tp'), may hold values from -6 to 6
- span_token_values: bfloat16 [2048, 1024], P('req', 'tp'), may hold values from -6 to 6
- cache_keys: bfloat16 [16384, 1024], P('req', 'tp'), may hold values from -6 to 6
- prompt_cache_values: bfloat16 [16384, 1024], P('req', 'tp'), may hold values from -6 to 6
- lengths: int32 [2], replicated, may hold values from 2 to 8192, as said below
Outputs:
- attention: bfloat16 [2048, 8192], P(('req', 'tp'))
The draws below stay inside these ranges and needn't reach their ends.
Inputs may be any that keep to these rules, and one draw needn't show every extreme that they name: `lengths`: each group's cached prompt length; one group's is exactly 8192.
All inputs are finite; a program needn't handle non-finite values.
Results may differ from the reference program's by a relative error of at most 0.0045.
Values may be sent and summed in bfloat16 or wider, within the bound.
A program may use at most 128 MiB of HBM per device.

```python
import math
import jax
import jax.numpy as jnp
from jax import lax

QUERY_HEADS = 64
KEY_VALUE_HEADS = 8
HEAD_SIZE = 128
SPAN_TOKENS = 1024
REQUEST_GROUPS = 2
ALL_SPAN_TOKENS = 2048
MAX_PROMPT_ROWS = 8192


def draw_queries(key, part):
    value_rows_joined = jnp.clip(jax.random.normal(jax.random.fold_in(key, 1), (ALL_SPAN_TOKENS, QUERY_HEADS * HEAD_SIZE), jnp.float32) * 3.5, -16.0, 16.0)
    return value_rows_joined.astype(jnp.bfloat16)


def draw_cache_keys(key, part):
    value_rows_joined = jnp.clip(jax.random.normal(jax.random.fold_in(key, 2), (REQUEST_GROUPS * MAX_PROMPT_ROWS, KEY_VALUE_HEADS * HEAD_SIZE), jnp.float32), -6.0, 6.0)
    return value_rows_joined.astype(jnp.bfloat16)


def draw_lengths(key, part):
    drawn = jax.random.randint(jax.random.fold_in(key, 3), (REQUEST_GROUPS,), 2, MAX_PROMPT_ROWS + 1, dtype=jnp.int32)
    longest = jax.random.randint(jax.random.fold_in(key, 4), (), 0, REQUEST_GROUPS, dtype=jnp.int32)
    return jnp.where(jnp.arange(REQUEST_GROUPS, dtype=jnp.int32) == longest, MAX_PROMPT_ROWS, drawn).astype(jnp.int32)


def steps_of(rng, extent, cuts, least, top_value):
    def one(dim, shards_of):
        draws = jax.random.uniform(jax.random.fold_in(jax.random.fold_in(rng, 6), dim), (shards_of,), jnp.float32, least / len(cuts), top_value / len(cuts))
        return jnp.repeat(jnp.exp(draws), extent[dim] // shards_of).reshape((-1,) + (1,) * (len(extent) - dim - 1))

    level = one(*cuts[0])
    for cut in cuts[1:]:
        level = level * one(*cut)
    return level


def noise(rng, dims, scale, reach, shards=(), kind=jnp.bfloat16):
    entries = scale * jax.random.normal(rng, dims, jnp.float32)
    if shards:
        entries = entries * steps_of(rng, dims, shards, -0.22, 0.18)
    return jnp.clip(entries, -reach, reach).astype(kind)


def setup_inputs(seed: int = 0) -> dict:
    splits = jax.random.split(jax.random.key(seed), 7)
    return {
        "queries": draw_queries(jax.random.fold_in(splits[6], 71), 0),
        "span_rotated_keys": noise(splits[1], (ALL_SPAN_TOKENS, KEY_VALUE_HEADS * HEAD_SIZE), 1.0, 6.0, ((0, 16), (1, 2))),
        "span_token_values": noise(splits[2], (ALL_SPAN_TOKENS, KEY_VALUE_HEADS * HEAD_SIZE), 1.0, 6.0, ((0, 16), (1, 2))),
        "cache_keys": draw_cache_keys(jax.random.fold_in(splits[6], 71), 0),
        "prompt_cache_values": noise(splits[4], (REQUEST_GROUPS * MAX_PROMPT_ROWS, KEY_VALUE_HEADS * HEAD_SIZE), 1.0, 6.0, ((0, 16), (1, 2))),
        "lengths": draw_lengths(jax.random.fold_in(splits[6], 71), 0),
    }


NEG_FILL = -1e+30

def reference(queries, span_rotated_keys, span_token_values, cache_keys, prompt_cache_values, lengths):
    heads_per_group = QUERY_HEADS // KEY_VALUE_HEADS
    score_scale = 1.0 / math.sqrt(HEAD_SIZE)
    query_head_rows = queries.reshape(REQUEST_GROUPS, SPAN_TOKENS, KEY_VALUE_HEADS, heads_per_group, HEAD_SIZE).transpose(0, 2, 3, 1, 4)
    query_head_rows = query_head_rows.reshape(REQUEST_GROUPS * KEY_VALUE_HEADS * heads_per_group, SPAN_TOKENS, HEAD_SIZE)

    def key_layout(cached_rows, span_portion):
        joined_rows = jnp.concatenate([cached_rows.reshape(REQUEST_GROUPS, MAX_PROMPT_ROWS, KEY_VALUE_HEADS, HEAD_SIZE), span_portion.reshape(REQUEST_GROUPS, SPAN_TOKENS, KEY_VALUE_HEADS, HEAD_SIZE)], axis=1)
        return joined_rows.transpose(0, 2, 1, 3).reshape(REQUEST_GROUPS * KEY_VALUE_HEADS, MAX_PROMPT_ROWS + SPAN_TOKENS, HEAD_SIZE)
    all_keys = key_layout(cache_keys, span_rotated_keys)
    all_values = key_layout(prompt_cache_values, span_token_values)
    key_pos = jnp.arange(MAX_PROMPT_ROWS + SPAN_TOKENS, dtype=jnp.int32)
    query_pos = jnp.arange(SPAN_TOKENS, dtype=jnp.int32)

    def single_head(inputs):
        query_rows, head_index = inputs
        key_value_index = head_index // heads_per_group
        key_rows = lax.dynamic_index_in_dim(all_keys, key_value_index, 0, keepdims=False)
        value_rows = lax.dynamic_index_in_dim(all_values, key_value_index, 0, keepdims=False)
        group_length = lax.dynamic_index_in_dim(lengths, key_value_index // KEY_VALUE_HEADS, 0, keepdims=False)
        allowed = jnp.where(key_pos[None, :] < MAX_PROMPT_ROWS, key_pos[None, :] < group_length, key_pos[None, :] - MAX_PROMPT_ROWS <= query_pos[:, None])
        scores = jnp.dot(query_rows, key_rows.T, preferred_element_type=jnp.float32) * score_scale
        scores = jnp.where(allowed, scores, NEG_FILL)
        row_max = lax.optimization_barrier(jnp.max(scores, axis=-1, keepdims=True))
        weights = jnp.where(allowed, jnp.exp(scores - row_max), 0.0)
        row_total = lax.optimization_barrier(jnp.sum(weights, axis=-1, keepdims=True))
        numerator = jnp.dot(weights.astype(jnp.bfloat16), value_rows, preferred_element_type=jnp.float32)
        return (numerator / row_total).astype(jnp.bfloat16)
    per_head_outputs = lax.map(single_head, (query_head_rows, jnp.arange(REQUEST_GROUPS * KEY_VALUE_HEADS * heads_per_group, dtype=jnp.int32)))
    per_head_outputs = per_head_outputs.reshape(REQUEST_GROUPS, KEY_VALUE_HEADS, heads_per_group, SPAN_TOKENS, HEAD_SIZE).transpose(0, 3, 1, 2, 4)
    return per_head_outputs.reshape(REQUEST_GROUPS * SPAN_TOKENS, QUERY_HEADS * HEAD_SIZE)
```

```python
import functools
import math

import jax
import jax.numpy as jnp
from jax import lax
from jax.experimental import pallas as pl
from jax.experimental.pallas import tpu as pltpu
from jax.sharding import PartitionSpec as P

D = 128
KEY_BLOCK = 512
NEG_FILL = -1e30
LOG2_SCALE = math.log2(math.e) / math.sqrt(D)
MESH = pl.DeviceIdType.MESH


def kernel(
    n_tp,
    kv_heads,
    len_ref,
    q_ref,
    sk_ref,
    sv_ref,
    ck_ref,
    cv_ref,
    out_ref,
    q_buf,
    k_buf,
    kt_buf,
    v_buf,
    bias_buf,
    acc_buf,
    max_buf,
    part_out,
    part_in,
    lse_out,
    lse_in,
    merged,
    local_sem,
    kv_send,
    kv_recv,
    q_send,
    q_recv,
    part_send,
    part_recv,
    out_send,
    out_recv,
):
    tok = q_ref.shape[0]
    rows = ck_ref.shape[0]
    core_heads = q_buf.shape[2] // D
    width = core_heads * D
    kvh = k_buf.shape[0] // 2
    per_kv = core_heads // kvh
    part_width = per_kv * D
    pair_tok = 2 * tok
    cache = 2 * rows
    out_rows = out_ref.shape[0]

    r = lax.axis_index("req")
    t = lax.axis_index("tp")
    c = lax.rem(r, 2)
    x = lax.rem(lax.div(r, 2), 2)
    z = lax.rem(lax.div(r, 4), 2)
    g = lax.div(r, 8)

    def device(dz, dx, dc, dy=0):
        zz = 1 - z if dz else z
        xx = 1 - x if dx else x
        cc = 1 - c if dc else c
        return (g * 8 + zz * 4 + xx * 2 + cc, lax.rem(t + dy, n_tp) if dy else t)

    group_partners = [(0, 0, 1, 0), (0, 1, 0, 0), (0, 1, 1, 0), (1, 0, 0, 0), (1, 0, 1, 0)]
    out_partners = [(0, 0, 1, 0)]
    for dy in range(1, n_tp):
        out_partners += [(0, 0, 0, dy), (0, 0, 1, dy)]
    barrier = pltpu.get_barrier_semaphore()
    partners = group_partners + out_partners[1:]
    for partner in partners:
        pl.semaphore_signal(barrier, inc=1, device_id=device(*partner), device_id_type=MESH)

    for s in range(2 * kvh):
        v_buf[s, :, D:] = jnp.ones((cache + pair_tok, D), jnp.bfloat16)
    group_length = len_ref[g]
    for s in range(2):
        zz = z if s == 0 else 1 - z
        first = (zz * 4 + x * 2) * rows
        position = first + lax.broadcasted_iota(jnp.int32, (1, cache), 1)
        bias_buf[s] = jnp.where(position < group_length, 0.0, NEG_FILL)
    pl.semaphore_wait(barrier, len(partners))

    def kv_pieces(src, j, dest_core):
        col = j * D
        if kv_heads > 1:
            col = pl.multiple_of(dest_core * (kvh * D) + j * D, D)
        slot = src * kvh + j
        cache_at = pl.ds(pl.multiple_of(c * rows, 16), rows)
        span_at = pl.ds(pl.multiple_of(cache + c * tok, 16), tok)
        return [
            (ck_ref.at[:, pl.ds(col, D)], k_buf.at[slot, cache_at, :]),
            (sk_ref.at[:, pl.ds(col, D)], k_buf.at[slot, span_at, :]),
            (cv_ref.at[:, pl.ds(col, D)], v_buf.at[slot, cache_at, pl.ds(0, D)]),
            (sv_ref.at[:, pl.ds(col, D)], v_buf.at[slot, span_at, pl.ds(0, D)]),
        ]

    def q_piece(group_set, j, dest_core):
        col = pl.multiple_of(dest_core * width + j * part_width, D)
        return (
            q_ref.at[:, pl.ds(col, part_width)],
            q_buf.at[
                group_set, pl.ds(pl.multiple_of(c * tok, 16), tok), pl.ds(j * part_width, part_width)
            ],
        )

    def remote(pair, send, recv, dest):
        copy = pltpu.make_async_remote_copy(
            src_ref=pair[0],
            dst_ref=pair[1],
            send_sem=send,
            recv_sem=recv,
            device_id=dest,
            device_id_type=MESH,
        )
        copy.start()
        return copy

    locals_ = {}
    kv_copies = {}
    q_copies = {}

    def start_local(j):
        pairs = kv_pieces(0, j, c) + [q_piece(0, j, c)]
        copies = []
        for i, (src, dst) in enumerate(pairs):
            copy = pltpu.make_async_copy(src, dst, local_sem.at[j * 5 + i])
            copy.start()
            copies.append(copy)
        locals_[j] = copies

    def start_kv(way, j):
        dz, dc = ((0, 1), (1, 0), (1, 1))[way]
        pairs = kv_pieces(dz, j, 1 - c if dc else c)
        kv_copies[way, j] = [
            remote(
                pair,
                kv_send.at[(way * kvh + j) * 4 + i],
                kv_recv.at[(way * kvh + j) * 4 + i],
                device(dz, 0, dc),
            )
            for i, pair in enumerate(pairs)
        ]

    def start_q(way, j):
        dx, dc = ((0, 1), (1, 0), (1, 1))[way]
        q_copies[way, j] = remote(
            q_piece(dx, j, 1 - c if dc else c),
            q_send.at[way * kvh + j],
            q_recv.at[way * kvh + j],
            device(0, dx, dc),
        )

    for j in range(kvh):
        start_local(j)
        start_q(0, j)
        start_kv(0, j)
        start_q(1, j)
        start_q(2, j)
        start_kv(1, j)
        start_kv(2, j)

    def unit(group_set, src, j):
        slot = src * kvh + j
        q_first = (z * 4 + (x if group_set == 0 else 1 - x) * 2) * tok
        k_first = ((z if src == 0 else 1 - z) * 4 + x * 2) * tok
        ahead = (
            q_first
            - k_first
            + lax.broadcasted_iota(jnp.int32, (pair_tok, pair_tok), 0)
            - lax.broadcasted_iota(jnp.int32, (pair_tok, pair_tok), 1)
        )

        def one_head(h, carry):
            head = group_set * core_heads + j * per_kv + h
            q = q_buf[
                group_set, :, pl.ds(pl.multiple_of(j * part_width + h * D, D), D)
            ]
            run_max = acc = None
            if src == 1:
                run_max = max_buf[head][:, :1]
                acc = acc_buf[head]
            block = math.gcd(KEY_BLOCK, cache)
            spans = [(b * block, block) for b in range(cache // block)] + [(cache, pair_tok)]
            for start, size in spans:
                scores = (
                    jnp.dot(
                        q,
                        kt_buf[slot, :, start : start + size],
                        preferred_element_type=jnp.float32,
                    )
                    * LOG2_SCALE
                )
                if start < cache:
                    scores = scores + bias_buf[src, :, start : start + size]
                else:
                    scores = jnp.where(ahead >= 0, scores, NEG_FILL)
                top = jnp.max(scores, axis=1, keepdims=True)
                new_max = top if run_max is None else jnp.maximum(run_max, top)
                weights = jnp.exp2(scores - new_max).astype(jnp.bfloat16)
                term = jnp.dot(
                    weights,
                    v_buf[slot, start : start + size, :],
                    preferred_element_type=jnp.float32,
                )
                acc = term if run_max is None else acc * jnp.exp2(run_max - new_max) + term
                run_max = new_max
            if src == 1 and group_set == 1:
                total = acc[:, D : D + 1]
                part_out[j, :, pl.ds(pl.multiple_of(h * D, D), D)] = (acc[:, :D] / total).astype(
                    jnp.bfloat16
                )
                lane = lax.broadcasted_iota(jnp.int32, (pair_tok, D), 1)
                lse_out[j] = jnp.where(lane == h, run_max + jnp.log2(total), lse_out[j])
            else:
                acc_buf[head] = acc
                max_buf[head] = jnp.broadcast_to(run_max, (pair_tok, D))
            return carry

        lax.fori_loop(0, per_kv, one_head, 0)

    def turn_keys(src, j):
        slot = src * kvh + j
        kt_buf[slot] = k_buf[slot].T

    for j in range(kvh):
        lse_out[j] = jnp.zeros((pair_tok, D), jnp.float32)

    for j in range(kvh):
        for copy in locals_[j]:
            copy.wait()
        for copy in kv_copies[0, j] + [q_copies[0, j]]:
            copy.wait_recv()
        turn_keys(0, j)
        unit(0, 0, j)
    for j in range(kvh):
        q_copies[1, j].wait_recv()
        q_copies[2, j].wait_recv()
        unit(1, 0, j)
    part_copies = []
    for j in range(kvh):
        for copy in kv_copies[1, j] + kv_copies[2, j]:
            copy.wait_recv()
        turn_keys(1, j)
        unit(1, 1, j)
        for i, (src, dst) in enumerate(((part_out, part_in), (lse_out, lse_in))):
            part_copies.append(
                remote(
                    (src.at[j], dst.at[j]),
                    part_send.at[2 * j + i],
                    part_recv.at[2 * j + i],
                    device(0, 1, 0),
                )
            )
        unit(0, 1, j)
    out_copies = []
    out_locals = []
    for j in range(kvh):
        part_copies[2 * j].wait_recv()
        part_copies[2 * j + 1].wait_recv()

        def merge(h, carry):
            head = j * per_kv + h
            lane = lax.broadcasted_iota(jnp.int32, (pair_tok, D), 1)
            other = jnp.sum(jnp.where(lane == h, lse_in[j], 0.0), axis=1, keepdims=True)
            own_max = max_buf[head][:, :1]
            top = jnp.maximum(own_max, other)
            own = jnp.exp2(own_max - top)
            theirs = jnp.exp2(other - top)
            cols = pl.ds(pl.multiple_of(h * D, D), D)
            acc = acc_buf[head]
            total = acc[:, D : D + 1] * own + theirs
            value = acc[:, :D] * own + part_in[j, :, cols].astype(jnp.float32) * theirs
            merged[j, :, cols] = (value / total).astype(jnp.bfloat16)
            return carry

        lax.fori_loop(0, per_kv, merge, 0)
        col = pl.multiple_of(t * (2 * width) + c * width + j * part_width, D)
        for i, partner in enumerate([(0, 0, 0, 0)] + out_partners):
            dest = device(*partner)
            dest_core = 1 - c if partner[2] else c
            src = merged.at[
                j, pl.ds(pl.multiple_of(dest_core * tok + dest[1] * out_rows, 16), out_rows), :
            ]
            dst = out_ref.at[:, pl.ds(col, part_width)]
            if i == 0:
                copy = pltpu.make_async_copy(src, dst, local_sem.at[5 * kvh + j])
                copy.start()
                out_locals.append(copy)
            else:
                k = j * len(out_partners) + i - 1
                out_copies.append(remote((src, dst), out_send.at[k], out_recv.at[k], dest))

    for copy in out_locals:
        copy.wait()
    for copy in out_copies:
        copy.wait_recv()
    for copies in kv_copies.values():
        for copy in copies:
            copy.wait_send()
    for copy in list(q_copies.values()) + part_copies + out_copies:
        copy.wait_send()


def body(n_tp, queries, span_keys, span_values, cache_keys, cache_values, lengths):
    tok = queries.shape[0]
    rows = cache_keys.shape[0]
    kv_heads = cache_keys.shape[1] // D
    kvh = max(1, kv_heads // 2)
    core_heads = queries.shape[1] // D // 2
    part_width = core_heads // kvh * D
    pair_tok, keys = 2 * tok, 2 * (rows + tok)
    n_out = 1 + 2 * (n_tp - 1)
    dma = pltpu.SemaphoreType.DMA
    any_spec = pl.BlockSpec(memory_space=pl.ANY)
    return pl.pallas_call(
        functools.partial(kernel, n_tp, kv_heads),
        out_shape=jax.ShapeDtypeStruct((tok // n_tp, queries.shape[1] * n_tp), jnp.bfloat16),
        in_specs=[pl.BlockSpec(memory_space=pltpu.SMEM)] + [any_spec] * 5,
        out_specs=any_spec,
        scratch_shapes=[
            pltpu.VMEM((2, pair_tok, core_heads * D), jnp.bfloat16),
            pltpu.VMEM((2 * kvh, keys, D), jnp.bfloat16),
            pltpu.VMEM((2 * kvh, D, keys), jnp.bfloat16),
            pltpu.VMEM((2 * kvh, keys, 2 * D), jnp.bfloat16),
            pltpu.VMEM((2, 1, 2 * rows), jnp.float32),
            pltpu.VMEM((2 * core_heads, pair_tok, 2 * D), jnp.float32),
            pltpu.VMEM((2 * core_heads, pair_tok, D), jnp.float32),
            pltpu.VMEM((kvh, pair_tok, part_width), jnp.bfloat16),
            pltpu.VMEM((kvh, pair_tok, part_width), jnp.bfloat16),
            pltpu.VMEM((kvh, pair_tok, D), jnp.float32),
            pltpu.VMEM((kvh, pair_tok, D), jnp.float32),
            pltpu.VMEM((kvh, pair_tok, part_width), jnp.bfloat16),
            dma((6 * kvh,)),
            dma((12 * kvh,)),
            dma((12 * kvh,)),
            dma((3 * kvh,)),
            dma((3 * kvh,)),
            dma((2 * kvh,)),
            dma((2 * kvh,)),
            dma((n_out * kvh,)),
            dma((n_out * kvh,)),
        ],
        compiler_params=pltpu.CompilerParams(
            collective_id=0, has_side_effects=True, vmem_limit_bytes=52 << 20
        ),
        name="spanned_attention",
    )(lengths, queries, span_keys, span_values, cache_keys, cache_values)


def solution(mesh):
    in_specs = (P("req", "tp"), P("req", "tp"), P("req", "tp"), P("req", "tp"), P("req", "tp"), P())
    out_specs = P(("req", "tp"), None)
    return jax.shard_map(
        functools.partial(body, mesh.shape["tp"]),
        mesh=mesh,
        in_specs=in_specs,
        out_specs=out_specs,
        check_vma=False,
    )
```

```python
import functools
import math

import jax
import jax.numpy as jnp
from jax import lax
from jax.experimental import pallas as pl
from jax.experimental.pallas import tpu as pltpu
from jax.sharding import PartitionSpec as P

D = 128
KEY_BLOCK = 512
NEG_FILL = -1e30
LOG2_SCALE = math.log2(math.e) / math.sqrt(D)
MESH = pl.DeviceIdType.MESH


def kernel(
    n_tp,
    kv_heads,
    len_ref,
    q_ref,
    sk_ref,
    sv_ref,
    ck_ref,
    cv_ref,
    out_ref,
    q_buf,
    k_buf,
    kt_buf,
    v_buf,
    bias_buf,
    acc_buf,
    max_buf,
    part_out,
    part_in,
    lse_out,
    lse_in,
    merged,
    local_sem,
    kv_send,
    kv_recv,
    q_send,
    q_recv,
    part_send,
    part_recv,
    out_send,
    out_recv,
):
    tok = q_ref.shape[0]
    rows = ck_ref.shape[0]
    core_heads = q_buf.shape[2] // D
    width = core_heads * D
    kvh = k_buf.shape[0] // 2
    per_kv = core_heads // kvh
    part_width = per_kv * D
    pair_tok = 2 * tok
    cache = 2 * rows
    out_rows = out_ref.shape[0]

    r = lax.axis_index("req")
    t = lax.axis_index("tp")
    c = lax.rem(r, 2)
    x = lax.rem(lax.div(r, 2), 2)
    z = lax.rem(lax.div(r, 4), 2)
    g = lax.div(r, 8)

    def device(dz, dx, dc, dy=0):
        zz = 1 - z if dz else z
        xx = 1 - x if dx else x
        cc = 1 - c if dc else c
        return (g * 8 + zz * 4 + xx * 2 + cc, lax.rem(t + dy, n_tp) if dy else t)

    group_partners = [(0, 0, 1, 0), (0, 1, 0, 0), (0, 1, 1, 0), (1, 0, 0, 0), (1, 0, 1, 0)]
    out_partners = [(0, 0, 1, 0)]
    for dy in range(1, n_tp):
        out_partners += [(0, 0, 0, dy), (0, 0, 1, dy)]
    barrier = pltpu.get_barrier_semaphore()
    partners = group_partners + out_partners[1:]
    for partner in partners:
        pl.semaphore_signal(barrier, inc=1, device_id=device(*partner), device_id_type=MESH)

    for s in range(2 * kvh):
        v_buf[s, :, D:] = jnp.ones((cache + pair_tok, D), jnp.bfloat16)
    group_length = len_ref[g]
    for s in range(2):
        zz = z if s == 0 else 1 - z
        first = (zz * 4 + x * 2) * rows
        position = first + lax.broadcasted_iota(jnp.int32, (1, cache), 1)
        bias_buf[s] = jnp.where(position < group_length, 0.0, NEG_FILL)
    pl.semaphore_wait(barrier, len(partners))

    def kv_pieces(src, j, dest_core):
        col = j * D
        if kv_heads > 1:
            col = pl.multiple_of(dest_core * (kvh * D) + j * D, D)
        slot = src * kvh + j
        cache_at = pl.ds(pl.multiple_of(c * rows, 16), rows)
        span_at = pl.ds(pl.multiple_of(cache + c * tok, 16), tok)
        return [
            (ck_ref.at[:, pl.ds(col, D)], k_buf.at[slot, cache_at, :]),
            (sk_ref.at[:, pl.ds(col, D)], k_buf.at[slot, span_at, :]),
            (cv_ref.at[:, pl.ds(col, D)], v_buf.at[slot, cache_at, pl.ds(0, D)]),
            (sv_ref.at[:, pl.ds(col, D)], v_buf.at[slot, span_at, pl.ds(0, D)]),
        ]

    def q_piece(group_set, j, dest_core):
        col = pl.multiple_of(dest_core * width + j * part_width, D)
        return (
            q_ref.at[:, pl.ds(col, part_width)],
            q_buf.at[
                group_set, pl.ds(pl.multiple_of(c * tok, 16), tok), pl.ds(j * part_width, part_width)
            ],
        )

    def remote(pair, send, recv, dest):
        copy = pltpu.make_async_remote_copy(
            src_ref=pair[0],
            dst_ref=pair[1],
            send_sem=send,
            recv_sem=recv,
            device_id=dest,
            device_id_type=MESH,
        )
        copy.start()
        return copy

    locals_ = {}
    kv_copies = {}
    q_copies = {}

    def start_local(j):
        pairs = kv_pieces(0, j, c) + [q_piece(0, j, c)]
        copies = []
        for i, (src, dst) in enumerate(pairs):
            copy = pltpu.make_async_copy(src, dst, local_sem.at[j * 5 + i])
            copy.start()
            copies.append(copy)
        locals_[j] = copies

    def start_kv(way, j):
        dz, dc = ((0, 1), (1, 0), (1, 1))[way]
        pairs = kv_pieces(dz, j, 1 - c if dc else c)
        kv_copies[way, j] = [
            remote(
                pair,
                kv_send.at[(way * kvh + j) * 4 + i],
                kv_recv.at[(way * kvh + j) * 4 + i],
                device(dz, 0, dc),
            )
            for i, pair in enumerate(pairs)
        ]

    def start_q(way, j):
        dx, dc = ((0, 1), (1, 0), (1, 1))[way]
        q_copies[way, j] = remote(
            q_piece(dx, j, 1 - c if dc else c),
            q_send.at[way * kvh + j],
            q_recv.at[way * kvh + j],
            device(0, dx, dc),
        )

    for j in range(kvh):
        start_local(j)
        start_q(0, j)
        start_kv(0, j)
        start_q(1, j)
        start_q(2, j)
        start_kv(1, j)
        start_kv(2, j)

    def unit(group_set, src, j):
        slot = src * kvh + j
        q_first = (z * 4 + (x if group_set == 0 else 1 - x) * 2) * tok
        k_first = ((z if src == 0 else 1 - z) * 4 + x * 2) * tok
        ahead = (
            q_first
            - k_first
            + lax.broadcasted_iota(jnp.int32, (pair_tok, pair_tok), 0)
            - lax.broadcasted_iota(jnp.int32, (pair_tok, pair_tok), 1)
        )

        def one_head(h, carry):
            head = group_set * core_heads + j * per_kv + h
            q = q_buf[
                group_set, :, pl.ds(pl.multiple_of(j * part_width + h * D, D), D)
            ]
            run_max = acc = None
            if src == 1:
                run_max = max_buf[head][:, :1]
                acc = acc_buf[head]
            block = math.gcd(KEY_BLOCK, cache)
            spans = [(b * block, block) for b in range(cache // block)] + [(cache, pair_tok)]
            for start, size in spans:
                scores = (
                    jnp.dot(
                        q,
                        kt_buf[slot, :, start : start + size],
                        preferred_element_type=jnp.float32,
                    )
                    * LOG2_SCALE
                )
                if start < cache:
                    scores = scores + bias_buf[src, :, start : start + size]
                else:
                    scores = jnp.where(ahead >= 0, scores, NEG_FILL)
                top = jnp.max(scores, axis=1, keepdims=True)
                new_max = top if run_max is None else jnp.maximum(run_max, top)
                weights = jnp.exp2(scores - new_max).astype(jnp.bfloat16)
                term = jnp.dot(
                    weights,
                    v_buf[slot, start : start + size, :],
                    preferred_element_type=jnp.float32,
                )
                acc = term if run_max is None else acc * jnp.exp2(run_max - new_max) + term
                run_max = new_max
            if src == 1 and group_set == 1:
                total = acc[:, D : D + 1]
                part_out[j, :, pl.ds(pl.multiple_of(h * D, D), D)] = (acc[:, :D] / total).astype(
                    jnp.bfloat16
                )
                lane = lax.broadcasted_iota(jnp.int32, (pair_tok, D), 1)
                lse_out[j] = jnp.where(lane == h, run_max + jnp.log2(total), lse_out[j])
            else:
                acc_buf[head] = acc
                max_buf[head] = jnp.broadcast_to(run_max, (pair_tok, D))
            return carry

        lax.fori_loop(0, per_kv, one_head, 0, unroll=2)

    def turn_keys(src, j):
        slot = src * kvh + j
        kt_buf[slot] = k_buf[slot].T

    for j in range(kvh):
        lse_out[j] = jnp.zeros((pair_tok, D), jnp.float32)

    for j in range(kvh):
        for copy in locals_[j]:
            copy.wait()
        for copy in kv_copies[0, j] + [q_copies[0, j]]:
            copy.wait_recv()
        turn_keys(0, j)
        unit(0, 0, j)
    for j in range(kvh):
        q_copies[1, j].wait_recv()
        q_copies[2, j].wait_recv()
        unit(1, 0, j)
    part_copies = []
    for j in range(kvh):
        for copy in kv_copies[1, j] + kv_copies[2, j]:
            copy.wait_recv()
        turn_keys(1, j)
        unit(1, 1, j)
        for i, (src, dst) in enumerate(((part_out, part_in), (lse_out, lse_in))):
            part_copies.append(
                remote(
                    (src.at[j], dst.at[j]),
                    part_send.at[2 * j + i],
                    part_recv.at[2 * j + i],
                    device(0, 1, 0),
                )
            )
        unit(0, 1, j)
    out_copies = []
    out_locals = []
    for j in range(kvh):
        part_copies[2 * j].wait_recv()
        part_copies[2 * j + 1].wait_recv()

        def merge(h, carry):
            head = j * per_kv + h
            lane = lax.broadcasted_iota(jnp.int32, (pair_tok, D), 1)
            other = jnp.sum(jnp.where(lane == h, lse_in[j], 0.0), axis=1, keepdims=True)
            own_max = max_buf[head][:, :1]
            top = jnp.maximum(own_max, other)
            own = jnp.exp2(own_max - top)
            theirs = jnp.exp2(other - top)
            cols = pl.ds(pl.multiple_of(h * D, D), D)
            acc = acc_buf[head]
            total = acc[:, D : D + 1] * own + theirs
            value = acc[:, :D] * own + part_in[j, :, cols].astype(jnp.float32) * theirs
            merged[j, :, cols] = (value / total).astype(jnp.bfloat16)
            return carry

        lax.fori_loop(0, per_kv, merge, 0)
        col = pl.multiple_of(t * (2 * width) + c * width + j * part_width, D)
        for i, partner in enumerate([(0, 0, 0, 0)] + out_partners):
            dest = device(*partner)
            dest_core = 1 - c if partner[2] else c
            src = merged.at[
                j, pl.ds(pl.multiple_of(dest_core * tok + dest[1] * out_rows, 16), out_rows), :
            ]
            dst = out_ref.at[:, pl.ds(col, part_width)]
            if i == 0:
                copy = pltpu.make_async_copy(src, dst, local_sem.at[5 * kvh + j])
                copy.start()
                out_locals.append(copy)
            else:
                k = j * len(out_partners) + i - 1
                out_copies.append(remote((src, dst), out_send.at[k], out_recv.at[k], dest))

    for copy in out_locals:
        copy.wait()
    for copy in out_copies:
        copy.wait_recv()
    for copies in kv_copies.values():
        for copy in copies:
            copy.wait_send()
    for copy in list(q_copies.values()) + part_copies + out_copies:
        copy.wait_send()


def body(n_tp, queries, span_keys, span_values, cache_keys, cache_values, lengths):
    tok = queries.shape[0]
    rows = cache_keys.shape[0]
    kv_heads = cache_keys.shape[1] // D
    kvh = max(1, kv_heads // 2)
    core_heads = queries.shape[1] // D // 2
    part_width = core_heads // kvh * D
    pair_tok, keys = 2 * tok, 2 * (rows + tok)
    n_out = 1 + 2 * (n_tp - 1)
    dma = pltpu.SemaphoreType.DMA
    any_spec = pl.BlockSpec(memory_space=pl.ANY)
    return pl.pallas_call(
        functools.partial(kernel, n_tp, kv_heads),
        out_shape=jax.ShapeDtypeStruct((tok // n_tp, queries.shape[1] * n_tp), jnp.bfloat16),
        in_specs=[pl.BlockSpec(memory_space=pltpu.SMEM)] + [any_spec] * 5,
        out_specs=any_spec,
        scratch_shapes=[
            pltpu.VMEM((2, pair_tok, core_heads * D), jnp.bfloat16),
            pltpu.VMEM((2 * kvh, keys, D), jnp.bfloat16),
            pltpu.VMEM((2 * kvh, D, keys), jnp.bfloat16),
            pltpu.VMEM((2 * kvh, keys, 2 * D), jnp.bfloat16),
            pltpu.VMEM((2, 1, 2 * rows), jnp.float32),
            pltpu.VMEM((2 * core_heads, pair_tok, 2 * D), jnp.float32),
            pltpu.VMEM((2 * core_heads, pair_tok, D), jnp.float32),
            pltpu.VMEM((kvh, pair_tok, part_width), jnp.bfloat16),
            pltpu.VMEM((kvh, pair_tok, part_width), jnp.bfloat16),
            pltpu.VMEM((kvh, pair_tok, D), jnp.float32),
            pltpu.VMEM((kvh, pair_tok, D), jnp.float32),
            pltpu.VMEM((kvh, pair_tok, part_width), jnp.bfloat16),
            dma((6 * kvh,)),
            dma((12 * kvh,)),
            dma((12 * kvh,)),
            dma((3 * kvh,)),
            dma((3 * kvh,)),
            dma((2 * kvh,)),
            dma((2 * kvh,)),
            dma((n_out * kvh,)),
            dma((n_out * kvh,)),
        ],
        compiler_params=pltpu.CompilerParams(
            collective_id=0, has_side_effects=True, vmem_limit_bytes=52 << 20
        ),
        name="spanned_attention",
    )(lengths, queries, span_keys, span_values, cache_keys, cache_values)


def solution(mesh):
    in_specs = (P("req", "tp"), P("req", "tp"), P("req", "tp"), P("req", "tp"), P("req", "tp"), P())
    out_specs = P(("req", "tp"), None)
    return jax.shard_map(
        functools.partial(body, mesh.shape["tp"]),
        mesh=mesh,
        in_specs=in_specs,
        out_specs=out_specs,
        check_vma=False,
    )
```
